256 devices in a mesh: outer: 4 (over x_hi, core), dp: 64 (over y, x_lo, z).
Axes of the slice: x: 4 (x_hi: 2, x_lo: 2; x = x_hi * 2 + x_lo), y: 4, z: 8, core: 2. Of those that a mesh axis runs over, the one named last changes fastest.
Arguments:
- videos: bfloat16 [4096, 1024], P(('outer', 'dp'))
- captions: bfloat16 [131072, 1024], P(('outer', 'dp'))
- caption_owner: int32 [131072], P(('outer', 'dp')), may hold values from 0 to 4095, as said below
- log_temp: float32 [1], replicated, may hold values from 2 to 2.8
- bias: float32 [1], replicated, may hold values from -6 to -3
Outputs:
- video_grad: float32 [4096, 1024], P(('outer', 'dp'))
- caption_grad: float32 [131072, 1024], P(('outer', 'dp'))
- scalars: float32 [3], replicated
The draws below stay inside these ranges and needn't reach their ends.
Inputs may be any that keep to these rules, and one draw needn't show every extreme that they name: Captions stand in video order: caption_owner never falls, every video owns between 24 and 40 consecutive captions, videos 2k and 2k+1 together own exactly 64 captions, and some video owns exactly 40.
All inputs are finite; a program needn't handle non-finite values.
Results may differ from the reference program's by a relative error of at most 0.0023.
Values may be sent and summed in bfloat16 or wider, within the bound.
A program may use at most 128 MiB of HBM per device.

```python
import math
import jax
import jax.numpy as jnp
from jax import lax

D = 1024
MOST = 40
VIDEOS = 4096
CAPS = 131072


def shared_layout(key):
    per_video = CAPS // VIDEOS
    reach_most = MOST - per_video
    pair_count = VIDEOS // 2
    key_list = jax.random.split(jax.random.fold_in(key, 7), 4)
    pair_shift = jax.random.randint(key_list[0], (pair_count,), -reach_most, reach_most + 1)
    forced_pair = jax.random.randint(key_list[1], (), 0, pair_count)
    flip_sign = 2 * jax.random.randint(key_list[2], (), 0, 2) - 1
    pair_shift = jnp.where(jnp.arange(pair_count) == forced_pair, flip_sign * reach_most, pair_shift)
    lengths = jnp.stack([per_video + pair_shift, per_video - pair_shift], axis=1).reshape(VIDEOS)
    owners = jnp.repeat(jnp.arange(VIDEOS, dtype=jnp.int32), lengths, total_repeat_length=CAPS)
    cluster = jax.random.randint(key_list[3], (VIDEOS,), 0, VIDEOS // 8)
    return (owners.astype(jnp.int32), cluster)


def shared_parts(key):
    key_list = jax.random.split(jax.random.fold_in(key, 11), 2)
    centres = jax.random.normal(key_list[0], (VIDEOS // 8, D), jnp.float32)
    private = jax.random.normal(key_list[1], (VIDEOS, D), jnp.float32)
    return (centres, private)


def draw_caption_owner(key, part):
    owners, cluster = shared_layout(key)
    return owners


def draw_videos(key, part):
    owners, cluster = shared_layout(key)
    centres, private = shared_parts(key)
    key = jax.random.fold_in(key, 21)
    noise_key = jax.random.fold_in(key, 0)
    noise_part = jax.random.normal(noise_key, (VIDEOS, D), jnp.float32)
    values = 0.632 * centres[cluster] + 0.548 * private + 0.548 * noise_part
    return (0.2 * values).astype(jnp.bfloat16)


def draw_captions(key, part):
    owners, cluster = shared_layout(key)
    centres, private = shared_parts(key)
    key = jax.random.fold_in(key, 31)
    noise_key = jax.random.fold_in(key, 0)
    caption_cluster = cluster[owners]
    noise_part = jax.random.normal(noise_key, (CAPS, D), jnp.float32)
    values = 0.632 * centres[caption_cluster] + 0.548 * private[owners] + 0.548 * noise_part
    return (0.2 * values).astype(jnp.bfloat16)


def setup_inputs(seed: int = 0) -> dict:
    splits = jax.random.split(jax.random.key(seed), 6)
    return {
        "videos": draw_videos(jax.random.fold_in(splits[5], 71), 0),
        "captions": draw_captions(jax.random.fold_in(splits[5], 71), 0),
        "caption_owner": draw_caption_owner(jax.random.fold_in(splits[5], 71), 0),
        "log_temp": jnp.clip(jax.random.uniform(splits[3], (1,), jnp.float32, 2.0, 2.8), 2.0, 2.8),
        "bias": jnp.clip(jax.random.uniform(splits[4], (1,), jnp.float32, -6.0, -3.0), -6.0, -3.0),
    }


def unit_rows(values):
    widened = values.astype(jnp.float32)
    row_scale = lax.rsqrt(lax.optimization_barrier(jnp.sum(widened * widened, axis=1, keepdims=True)) + 1e-06)
    return (row_scale, widened * row_scale)

def back_rows(row_scale, unit_vals, incoming):
    return row_scale * (incoming - unit_vals * lax.optimization_barrier(jnp.sum(unit_vals * incoming, axis=1, keepdims=True)))

def reference(videos, captions, caption_owner, log_temp, bias):
    video_scale, video_unit = unit_rows(videos)
    video_low = video_unit.astype(jnp.bfloat16)
    caption_scale, caption_unit = unit_rows(captions)
    caption_low = caption_unit.astype(jnp.bfloat16)
    temper = jnp.exp(log_temp[0])
    bias_value = bias[0]
    block_size = math.gcd(VIDEOS, 512)
    block_count = VIDEOS // block_size
    video_blocks = video_low.reshape(block_count, block_size, D)

    def one_block(running, entry):
        cap_sum, totals = running
        block_index, block_rows = entry
        video_ids = block_index * block_size + jnp.arange(block_size, dtype=jnp.int32)
        logits = temper * jnp.dot(block_rows, caption_low.T, preferred_element_type=jnp.float32) + bias_value
        signs = jnp.where(caption_owner[None, :] == video_ids[:, None], 1.0, -1.0)
        pair_grad = -signs * jax.nn.sigmoid(-signs * logits)
        pair_low = pair_grad.astype(jnp.bfloat16)
        video_part = jnp.dot(pair_low, caption_low, preferred_element_type=jnp.float32)
        cap_sum = cap_sum + jnp.dot(pair_low.T, block_rows, preferred_element_type=jnp.float32)
        block_sums = jnp.stack([jnp.sum(-jax.nn.log_sigmoid(signs * logits)), jnp.sum(pair_grad * (logits - bias_value)), jnp.sum(pair_grad)])
        return ((cap_sum, totals + block_sums), video_part)
    start_state = (jnp.zeros((CAPS, D), jnp.float32), jnp.zeros((3,), jnp.float32))
    (cap_sum, totals), video_parts = lax.scan(one_block, start_state, (jnp.arange(block_count, dtype=jnp.int32), video_blocks))
    unit_video_grad = temper * video_parts.reshape(VIDEOS, D)
    unit_caption_grad = temper * cap_sum
    video_grad = back_rows(video_scale, video_unit, unit_video_grad)
    caption_grad = back_rows(caption_scale, caption_unit, unit_caption_grad)
    scalars = totals / (float(VIDEOS) * float(CAPS))
    return (video_grad, caption_grad, scalars)
```

```python
import jax
import jax.numpy as jnp
from jax import lax
from jax.experimental import pallas as pl
from jax.experimental.pallas import tpu as pltpu
from jax.sharding import PartitionSpec as P

MESH = pl.DeviceIdType.MESH
F32 = jnp.float32
BF16 = jnp.bfloat16
LOG2E = 1.4426950408889634
D = 1024
OWN = 16
CAP = 512
ALL = 4 * CAP
COPIES = 96


def device_at(x, y, z, core):
    return ((x // 2) * 2 + core, (y * 2 + x % 2) * 8 + z)


def kernel(
    videos, captions, owner, log_temp, bias,
    video_out, caption_out, scalar_out,
    G, C, V, PR, VA, VB, FA, FB,
    R1, RU, RM, TM, TP, RP, S2, TZ, RZ,
    TN1, RN1, TN2, RN2, TS, RS, CG, SC,
    send_sem, recv_sem,
):
    outer, inner = lax.axis_index("outer"), lax.axis_index("dp")
    x = (outer // 2) * 2 + (inner // 8) % 2
    y = inner // 16
    z = inner % 8
    core = outer % 2
    zh, zp = z // 2, z % 2

    def at(dx=0, dy=0, dz=0, other=False):
        return device_at(
            (x + dx + 4) % 4, (y + dy + 4) % 4, (z + dz + 8) % 8, 1 - core if other else core
        )

    started = []

    def send(src, dst, device):
        index = len(started)
        copy = pltpu.make_async_remote_copy(
            src_ref=src, dst_ref=dst, send_sem=send_sem.at[index], recv_sem=recv_sem.at[index],
            device_id=device, device_id_type=MESH,
        )
        copy.start()
        started.append(copy)
        return copy

    partners = [at(dx=i) for i in (1, 2, 3)] + [at(dy=i) for i in (1, 2, 3)]
    partners += [at(dz=i) for i in (1, 2, 4, 6, 7)] + [at(other=True)]
    barrier = pltpu.get_barrier_semaphore()
    for device in partners:
        pl.semaphore_signal(barrier, inc=1, device_id=device, device_id_type=MESH)

    temper = jnp.exp(jnp.full((1, 1), log_temp[0], F32))
    bias_value = bias[0]

    wide = videos[...].astype(F32)
    video_scale = lax.rsqrt(jnp.sum(wide * wide, axis=1, keepdims=True) + 1e-06)
    own_rows = pl.ds(pl.multiple_of(zh * OWN, OWN), OWN)
    G[x, y, own_rows, :] = (wide * video_scale).astype(BF16)

    pl.semaphore_wait(barrier, len(partners))

    mine = G.at[x, y, own_rows]
    along_z = [send(mine, mine, at(dz=2 * i)) for i in (1, 2, 3)]

    def low_captions(i, carry):
        rows = pl.ds(pl.multiple_of(i * 128, 128), 128)
        block = captions[rows, :].astype(F32)
        scale = lax.rsqrt(jnp.sum(block * block, axis=1, keepdims=True) + 1e-06)
        C[rows, :] = (block * scale).astype(BF16)
        return carry

    lax.fori_loop(0, CAP // 128, low_captions, 0)
    cap_up = send(C.at[0:256], C.at[1024:1280], at(dz=1))
    cap_down = send(C.at[256:512], C.at[1280:1536], at(dz=-1))
    cap_side = send(C.at[0:512], C.at[512:1024], at(other=True))

    for copy in along_z:
        copy.wait_recv()

    def unit_a(px, py, lo=0, hi=32):
        return G.at[(px + 4) % 4, (py + 4) % 4, lo:hi]

    def unit_b(px, py, lo=32, hi=64):
        return G.at[(px + 4) % 4, (py + 4) % 4, lo:hi]

    def same(unit, device):
        return send(unit, unit, device)

    ax_p, ax_m, by_p, by_m = {}, {}, {}, {}
    ax_p[0] = same(unit_a(x, y), at(dx=1))
    by_p[0] = same(unit_b(x, y), at(dy=1))
    ax_m[0] = same(unit_a(x, y), at(dx=-1))
    by_m[0] = same(unit_b(x, y), at(dy=-1))
    a_y, b_x = {}, {}
    for i in (1, 3, 2):
        a_y[i] = same(unit_a(x, y), at(dy=i))
        b_x[i] = same(unit_b(x, y), at(dx=i))
    for i in (1, 3, 2):
        a_y[i].wait_recv()
        ax_p[i] = same(unit_a(x, y - i), at(dx=1))
        ax_m[i] = same(unit_a(x, y - i), at(dx=-1))
        b_x[i].wait_recv()
        by_p[i] = same(unit_b(x - i, y), at(dy=1))
        by_m[i] = same(unit_b(x - i, y), at(dy=-1))
    far = []
    for i in (0, 1, 3, 2):
        ax_p[i].wait_recv()
        far.append(same(unit_a(x - 1, y - i, 0, 16), at(dx=1)))
        ax_m[i].wait_recv()
        far.append(same(unit_a(x + 1, y - i, 16, 32), at(dx=-1)))
        by_p[i].wait_recv()
        far.append(same(unit_b(x - i, y - 1, 32, 48), at(dy=1)))
        by_m[i].wait_recv()
        far.append(same(unit_b(x - i, y + 1, 48, 64), at(dy=-1)))
    cap_up.wait_recv()
    relay_up = send(C.at[1024:1280], C.at[1536:1792], at(other=True))
    cap_down.wait_recv()
    relay_down = send(C.at[1280:1536], C.at[1792:2048], at(other=True))
    cap_side.wait_recv()
    relay_up.wait_recv()
    relay_down.wait_recv()
    for copy in far:
        copy.wait_recv()

    slope = temper * LOG2E
    offset = bias_value * LOG2E

    def pair_step(k, sums):
        xk, yk = (x + k) % 4, (y + k) % 4
        for i in range(4):
            V[k * 256 + i * 32 : k * 256 + i * 32 + 32, :] = G[xk, i, 0:32, :]
            V[k * 256 + 128 + i * 32 : k * 256 + 128 + i * 32 + 32, :] = G[i, yk, 32:64, :]

        def columns(j, carry):
            total, logs = carry
            cols = pl.ds(pl.multiple_of(j * 512, 512), 512)
            dots = lax.dot_general(
                V[k * 256 : k * 256 + 256, :], C[cols, :], (((1,), (1,)), ((), ())),
                preferred_element_type=F32,
            )
            grown = jnp.exp2(dots * slope + offset)
            above = 1.0 + grown
            pairs = grown * pl.reciprocal(above, approx=False)
            PR[k * 256 : k * 256 + 256, cols] = pairs.astype(BF16)
            total = total + jnp.sum(pairs.reshape(32, 8, 512), axis=0)
            quads = above.reshape(8, 4, 8, 512)
            quads = (quads[:, 0] * quads[:, 1]) * (quads[:, 2] * quads[:, 3])
            logs = logs + jnp.sum(jnp.log(quads), axis=0)
            return total, logs

        return lax.fori_loop(0, 4, columns, sums)

    def own_pairs(sums):
        total, logs = sums
        dots = lax.dot_general(
            G[x, y, own_rows, :], C[0:512, :], (((1,), (1,)), ((), ())), preferred_element_type=F32
        )
        grown = jnp.exp2(dots * slope + offset)
        part = pl.reciprocal(1.0 + grown, approx=False)
        first = (outer * 64 + inner) * OWN
        ids = first + lax.broadcasted_iota(jnp.int32, (OWN, CAP), 0)
        match = owner[...] == ids
        pairs = jnp.where(match, -part, grown * part)
        row = jnp.where(zh < 2, y * 32 + zh * 16, 128 + x * 32 + (zh - 2) * 16)
        PR[pl.ds(pl.multiple_of(row, 16), 16), 0:512] = pairs.astype(BF16)
        logits = dots * temper + bias_value
        ones = jnp.where(match, 1.0, 0.0)
        taken = jnp.where(match, logits, 0.0)
        total = total - (ones[0:8] + ones[8:16])
        logs = logs - (taken[0:8] + taken[8:16])
        return total, logs

    def video_step(k, keep, power):
        def columns(j, carry):
            cols = pl.ds(pl.multiple_of(j * 256, 256), 256)
            part = jnp.dot(
                PR[k * 256 : k * 256 + 256, :], C[:, cols], preferred_element_type=F32
            )
            with_video = part * V[k * 256 : k * 256 + 256, cols].astype(F32)
            carry = carry + jnp.sum(with_video.reshape(32, 8, 256), axis=0)
            for i in range(4):
                piece_a = part[i * 32 : i * 32 + 32]
                piece_b = part[128 + i * 32 : 128 + i * 32 + 32]
                if keep:
                    FA[i, :, cols] = piece_a
                    FB[i, :, cols] = piece_b
                else:
                    VA[k - 1, i, :, cols] = piece_a.astype(BF16)
                    VB[k - 1, i, :, cols] = piece_b.astype(BF16)
            return carry

        return lax.fori_loop(0, 4, columns, power)

    sums = (jnp.zeros((8, 512), F32), jnp.zeros((8, 512), F32))
    power = jnp.zeros((8, 256), F32)

    sums = pair_step(2, sums)
    power = video_step(2, False, power)
    first_hop = [
        send(VA.at[1, :, 0:16], R1.at[0], at(dx=1)),
        send(VB.at[1, :, 0:16], R1.at[2], at(dy=1)),
        send(VA.at[1, :, 16:32], R1.at[1], at(dx=-1)),
        send(VB.at[1, :, 16:32], R1.at[3], at(dy=-1)),
    ]
    sums = pair_step(1, sums)
    power = video_step(1, False, power)
    plain = [
        send(VA.at[0, :, 16:32], RU.at[0], at(dx=1)),
        send(VB.at[0, :, 16:32], RU.at[2], at(dy=1)),
    ]
    sums = pair_step(3, sums)
    power = video_step(3, False, power)
    plain += [
        send(VA.at[2, :, 0:16], RU.at[1], at(dx=-1)),
        send(VB.at[2, :, 0:16], RU.at[3], at(dy=-1)),
    ]
    merged = []
    for n, (ref, k, lo, device) in enumerate(
        (
            (VA, 0, 0, at(dx=1)),
            (VA, 2, 16, at(dx=-1)),
            (VB, 0, 0, at(dy=1)),
            (VB, 2, 16, at(dy=-1)),
        )
    ):
        first_hop[(0, 2, 1, 3)[n]].wait_recv()
        for i in range(4):
            TM[n, i] = (ref[k, i, lo : lo + 16, :].astype(F32) + R1[n, i].astype(F32)).astype(BF16)
        merged.append(send(TM.at[n], RM.at[n], device))
    sums = pair_step(0, sums)
    sums = own_pairs(sums)
    power = video_step(0, True, power)

    row_of = lax.broadcasted_iota(jnp.int32, (8, 128), 0)
    SC[0] = jnp.where(
        row_of == 0,
        jnp.sum(sums[1]),
        jnp.where(row_of == 1, jnp.sum(power), jnp.sum(sums[0])),
    )

    def scalar_send(stage, first_slot, devices):
        return [
            send(SC.at[stage], SC.at[first_slot + n], device) for n, device in enumerate(devices)
        ]

    def scalar_take(stage, first_slot, copies):
        value = SC[stage]
        for n, copy in enumerate(copies):
            copy.wait_recv()
            value = value + SC[first_slot + n]
        SC[stage + 1] = value

    sc_x = scalar_send(0, 8, [at(dx=i) for i in (1, 2, 3)])

    def caption_part(first):
        return lax.dot_general(
            PR[:, first : first + 256], V[...], (((0,), (0,)), ((), ())),
            preferred_element_type=F32,
        )

    for i in range(2):
        TN1[i * 256 : i * 256 + 256, :] = caption_part(1536 + i * 256).astype(BF16)
    side_near = send(TN1, RN1, at(other=True))

    for copy in plain + merged:
        copy.wait_recv()
    for i in range(4):
        for ref, n in ((FA, 0), (FB, 2)):
            low = ref[i, 0:16, :] + RM[n, i].astype(F32) + RU[n + 1, i].astype(F32)
            high = ref[i, 16:32, :] + RU[n, i].astype(F32) + RM[n + 1, i].astype(F32)
            ref[i, 0:16, :] = low
            ref[i, 16:32, :] = high
            TP[n // 2, i, 0:16, :] = low.astype(BF16)
            TP[n // 2, i, 16:32, :] = high.astype(BF16)
    second_a, second_b = [], []
    for i in (1, 3, 2):
        second_a.append(send(TP.at[0, (y + i) % 4], RP.at[0, i - 1], at(dy=i)))
        second_b.append(send(TP.at[1, (x + i) % 4], RP.at[1, i - 1], at(dx=i)))
    scalar_take(0, 8, sc_x)
    sc_y = scalar_send(1, 11, [at(dy=i) for i in (1, 2, 3)])

    near = [caption_part(1024 + i * 256) for i in range(2)]
    side_near.wait_recv()
    for i in range(2):
        rows = slice(i * 256, i * 256 + 256)
        TN2[rows, :] = (near[i] + RN1[rows, :].astype(F32)).astype(BF16)
    back_down = send(TN2.at[0:256], RN2.at[0:256], at(dz=-1))
    back_up = send(TN2.at[256:512], RN2.at[256:512], at(dz=1))

    for copy in second_a + second_b:
        copy.wait_recv()
    sum_a = FA[y] + RP[0, 0].astype(F32) + RP[0, 1].astype(F32) + RP[0, 2].astype(F32)
    sum_b = FB[x] + RP[1, 0].astype(F32) + RP[1, 1].astype(F32) + RP[1, 2].astype(F32)
    for i, value in enumerate((sum_a[0:16], sum_a[16:32], sum_b[0:16], sum_b[16:32])):
        S2[i] = value
        TZ[i] = value.astype(BF16)
    third = [send(TZ.at[(zh + i) % 4], RZ.at[i - 1], at(dz=2 * i)) for i in (1, 2, 3)]
    scalar_take(1, 11, sc_y)
    sc_z = scalar_send(2, 14, [at(dz=2 * i) for i in (1, 2, 3)])

    for i in range(2):
        TS[i * 256 : i * 256 + 256, :] = caption_part(512 + i * 256).astype(BF16)
    side = send(TS, RS, at(other=True))
    scalar_take(2, 14, sc_z)
    sc_p = scalar_send(3, 17, [device_at(x, y, zh * 2 + 1 - zp, core)])
    for i in range(2):
        CG[i * 256 : i * 256 + 256, :] = caption_part(i * 256)
    scalar_take(3, 17, sc_p)
    sc_c = scalar_send(4, 18, [at(other=True)])

    for copy in third:
        copy.wait_recv()
    wide = videos[...].astype(F32)
    video_scale = lax.rsqrt(jnp.sum(wide * wide, axis=1, keepdims=True) + 1e-06)
    unit = wide * video_scale
    grad = temper * (
        S2[zh] + RZ[0].astype(F32) + RZ[1].astype(F32) + RZ[2].astype(F32)
    )
    video_out[...] = video_scale * (grad - unit * jnp.sum(unit * grad, axis=1, keepdims=True))

    scalar_take(4, 18, sc_c)
    scale_of = jnp.where(row_of == 1, jnp.broadcast_to(temper, (8, 128)), 1.0)
    scalar_out[...] = SC[5] * scale_of * (1.0 / 536870912.0)

    side.wait_recv()
    back_down.wait_recv()
    back_up.wait_recv()

    def finish(i, carry):
        rows = pl.ds(pl.multiple_of(i * 64, 64), 64)
        block = captions[rows, :].astype(F32)
        scale = lax.rsqrt(jnp.sum(block * block, axis=1, keepdims=True) + 1e-06)
        unit = block * scale
        grad = temper * (CG[rows, :] + RS[rows, :].astype(F32) + RN2[rows, :].astype(F32))
        caption_out[rows, :] = scale * (grad - unit * jnp.sum(unit * grad, axis=1, keepdims=True))
        return carry

    lax.fori_loop(0, CAP // 64, finish, 0)
    for copy in started:
        copy.wait_send()


def on_device(videos, captions, caption_owner, log_temp, bias):
    vmem = pl.BlockSpec(memory_space=pltpu.VMEM)
    smem = pl.BlockSpec(memory_space=pltpu.SMEM)
    V = pltpu.VMEM
    video_grad, caption_grad, scalars = pl.pallas_call(
        kernel,
        out_shape=(
            jax.ShapeDtypeStruct((OWN, D), F32),
            jax.ShapeDtypeStruct((CAP, D), F32),
            jax.ShapeDtypeStruct((8, 128), F32),
        ),
        in_specs=[vmem, vmem, vmem, smem, smem],
        out_specs=(vmem, vmem, vmem),
        scratch_shapes=[
            V((4, 4, 64, D), BF16),
            V((ALL, D), BF16),
            V((1024, D), BF16),
            V((1024, ALL), BF16),
            V((3, 4, 32, D), BF16),
            V((3, 4, 32, D), BF16),
            V((4, 32, D), F32),
            V((4, 32, D), F32),
            V((4, 4, 16, D), BF16),
            V((4, 4, 16, D), BF16),
            V((4, 4, 16, D), BF16),
            V((4, 4, 16, D), BF16),
            V((2, 4, 32, D), BF16),
            V((2, 3, 32, D), BF16),
            V((4, OWN, D), F32),
            V((4, OWN, D), BF16),
            V((3, OWN, D), BF16),
            V((CAP, D), BF16),
            V((CAP, D), BF16),
            V((CAP, D), BF16),
            V((CAP, D), BF16),
            V((CAP, D), BF16),
            V((CAP, D), BF16),
            V((CAP, D), F32),
            V((19, 8, 128), F32),
            pltpu.SemaphoreType.DMA((COPIES,)),
            pltpu.SemaphoreType.DMA((COPIES,)),
        ],
        compiler_params=pltpu.CompilerParams(
            collective_id=0, has_side_effects=True, vmem_limit_bytes=56 * 2**20
        ),
        cost_estimate=pl.CostEstimate(
            flops=3 * 2 * 1024 * ALL * D, bytes_accessed=4 * 2**20, transcendentals=3 * 1024 * ALL
        ),
    )(videos, captions, caption_owner.reshape(1, CAP), log_temp, bias)
    return video_grad, caption_grad, scalars[:3, 0]


def solution(mesh):
    in_specs = (P(("outer", "dp"), None), P(("outer", "dp"), None), P(("outer", "dp")), P(), P())
    out_specs = (P(("outer", "dp"), None), P(("outer", "dp"), None), P())
    return jax.shard_map(
        on_device, mesh=mesh, in_specs=in_specs, out_specs=out_specs, check_vma=False
    )
```

```python
import jax
import jax.numpy as jnp
from jax import lax
from jax.experimental import pallas as pl
from jax.experimental.pallas import tpu as pltpu
from jax.sharding import PartitionSpec as P

MESH = pl.DeviceIdType.MESH
F32 = jnp.float32
BF16 = jnp.bfloat16
LOG2E = 1.4426950408889634
D = 1024
OWN = 16
CAP = 512
ALL = 4 * CAP
COPIES = 96


def device_at(x, y, z, core):
    return ((x // 2) * 2 + core, (y * 2 + x % 2) * 8 + z)


def kernel(
    videos_far, captions_far, owner_far, log_temp, bias,
    video_out, caption_out, scalar_out,
    G, C, V, PR, VA, VB, FA, FB,
    RA, RB, TP, RP, S2, TZ, RZ,
    TN1, RN1, TN2, RN2, TS, RS, CG, SC,
    videos, captions, owner, send_sem, recv_sem, local_sem,
):
    outer, inner = lax.axis_index("outer"), lax.axis_index("dp")
    x = (outer // 2) * 2 + (inner // 8) % 2
    y = inner // 16
    z = inner % 8
    core = outer % 2
    zh, zp = z // 2, z % 2

    def at(dx=0, dy=0, dz=0, other=False):
        return device_at(
            (x + dx + 4) % 4, (y + dy + 4) % 4, (z + dz + 8) % 8, 1 - core if other else core
        )

    started = []

    def send(src, dst, device):
        index = len(started)
        copy = pltpu.make_async_remote_copy(
            src_ref=src, dst_ref=dst, send_sem=send_sem.at[index], recv_sem=recv_sem.at[index],
            device_id=device, device_id_type=MESH,
        )
        copy.start()
        started.append(copy)
        return copy

    partners = [at(dx=i) for i in (1, 2, 3)] + [at(dy=i) for i in (1, 2, 3)]
    partners += [at(dz=i) for i in (1, 2, 4, 6, 7)] + [at(other=True)]
    barrier = pltpu.get_barrier_semaphore()
    for device in partners:
        pl.semaphore_signal(barrier, inc=1, device_id=device, device_id_type=MESH)

    bring_videos = pltpu.make_async_copy(videos_far, videos, local_sem.at[8])
    bring_videos.start()
    bring = []
    for i in range(4):
        rows = pl.ds(i * 128, 128)
        bring.append(
            pltpu.make_async_copy(captions_far.at[rows], captions.at[rows], local_sem.at[i])
        )
    bring.append(pltpu.make_async_copy(owner_far, owner, local_sem.at[7]))
    for copy in bring:
        copy.start()
    temper = jnp.exp(jnp.full((1, 1), log_temp[0], F32))
    bias_value = bias[0]

    bring_videos.wait()
    wide = videos[...].astype(F32)
    video_scale = lax.rsqrt(jnp.sum(wide * wide, axis=1, keepdims=True) + 1e-06)
    own_rows = pl.ds(pl.multiple_of(zh * OWN, OWN), OWN)
    G[x, y, own_rows, :] = (wide * video_scale).astype(BF16)

    pl.semaphore_wait(barrier, len(partners))

    mine = G.at[x, y, own_rows]
    along_z = [send(mine, mine, at(dz=2 * i)) for i in (1, 2, 3)]
    def low_captions(i, carry):
        rows = pl.ds(pl.multiple_of(i * 128, 128), 128)
        block = captions[rows, :].astype(F32)
        scale = lax.rsqrt(jnp.sum(block * block, axis=1, keepdims=True) + 1e-06)
        C[rows, :] = (block * scale).astype(BF16)
        return carry

    for copy in bring:
        copy.wait()
    lax.fori_loop(0, CAP // 128, low_captions, 0)
    cap_up = send(C.at[0:256], C.at[1024:1280], at(dz=1))
    cap_down = send(C.at[256:512], C.at[1280:1536], at(dz=-1))
    cap_side = send(C.at[0:512], C.at[512:1024], at(other=True))
    for copy in along_z:
        copy.wait_recv()

    def unit_a(px, py, lo=0, hi=32):
        return G.at[(px + 4) % 4, (py + 4) % 4, lo:hi]

    def unit_b(px, py, lo=32, hi=64):
        return G.at[(px + 4) % 4, (py + 4) % 4, lo:hi]

    def same(unit, device):
        return send(unit, unit, device)

    ax_p, ax_m, by_p, by_m = {}, {}, {}, {}
    a_y, b_x = {}, {}
    for i in (2, 1, 3):
        a_y[i] = same(unit_a(x, y), at(dy=i))
        b_x[i] = same(unit_b(x, y), at(dx=i))
    ax_p[0] = same(unit_a(x, y), at(dx=1))
    by_p[0] = same(unit_b(x, y), at(dy=1))
    ax_m[0] = same(unit_a(x, y), at(dx=-1))
    by_m[0] = same(unit_b(x, y), at(dy=-1))
    for i in (1, 3, 2):
        a_y[i].wait_recv()
        ax_p[i] = same(unit_a(x, y - i), at(dx=1))
        ax_m[i] = same(unit_a(x, y - i), at(dx=-1))
        b_x[i].wait_recv()
        by_p[i] = same(unit_b(x - i, y), at(dy=1))
        by_m[i] = same(unit_b(x - i, y), at(dy=-1))
    far = []

    def pass_on(i):
        ax_p[i].wait_recv()
        far.append(same(unit_a(x - 1, y - i, 0, 16), at(dx=1)))
        ax_m[i].wait_recv()
        far.append(same(unit_a(x + 1, y - i, 16, 32), at(dx=-1)))
        by_p[i].wait_recv()
        far.append(same(unit_b(x - i, y - 1, 32, 48), at(dy=1)))
        by_m[i].wait_recv()
        far.append(same(unit_b(x - i, y + 1, 48, 64), at(dy=-1)))

    slope = temper * LOG2E
    offset = bias_value * LOG2E

    def collect(k):
        xk, yk = (x + k) % 4, (y + k) % 4
        for i in range(4):
            V[k * 256 + i * 32 : k * 256 + i * 32 + 32, :] = G[xk, i, 0:32, :]
            V[k * 256 + 128 + i * 32 : k * 256 + 128 + i * 32 + 32, :] = G[i, yk, 32:64, :]

    def pair_step(k, half, sums):
        total, logs, power = sums
        rows = slice(k * 256, k * 256 + 256)
        cols = slice(half * 1024, half * 1024 + 1024)
        dots = lax.dot_general(
            V[rows, :], C[cols, :], (((1,), (1,)), ((), ())), preferred_element_type=F32
        )
        grown = jnp.exp2(dots * slope + offset)
        above = 1.0 + grown
        pairs = grown * pl.reciprocal(above, approx=False)
        PR[rows, cols] = pairs.astype(BF16)
        total = total + jnp.sum(pairs.reshape(32, 8, 1024), axis=0)
        quads = above.reshape(8, 4, 8, 1024)
        quads = (quads[:, 0] * quads[:, 1]) * (quads[:, 2] * quads[:, 3])
        logs = logs + jnp.sum(jnp.log(quads), axis=0)
        power = power + jnp.sum((pairs * dots).reshape(32, 8, 1024), axis=0)
        return total, logs, power

    def own_pairs():
        dots = lax.dot_general(
            G[x, y, own_rows, :], C[0:512, :], (((1,), (1,)), ((), ())), preferred_element_type=F32
        )
        grown = jnp.exp2(dots * slope + offset)
        part = pl.reciprocal(1.0 + grown, approx=False)
        first = (outer * 64 + inner) * OWN
        ids = first + lax.broadcasted_iota(jnp.int32, (OWN, CAP), 0)
        match = owner[...] == ids
        pairs = jnp.where(match, -part, grown * part)
        row = jnp.where(zh < 2, y * 32 + zh * 16, 128 + x * 32 + (zh - 2) * 16)
        PR[pl.ds(pl.multiple_of(row, 16), 16), 0:512] = pairs.astype(BF16)
        logits = dots * temper + bias_value
        ones = jnp.where(match, 1.0, 0.0)
        taken = jnp.where(match, logits, 0.0)
        SC[20] = jnp.full((8, 128), jnp.sum(ones), F32)
        SC[21] = jnp.full((8, 128), jnp.sum(taken), F32)
        SC[22] = jnp.full((8, 128), jnp.sum(jnp.where(match, dots, 0.0)), F32)

    def video_step(k):
        part = jnp.dot(PR[k * 256 : k * 256 + 256, :], C[...], preferred_element_type=F32)
        for i in range(4):
            piece_a = part[i * 32 : i * 32 + 32]
            piece_b = part[128 + i * 32 : 128 + i * 32 + 32]
            if k == 0:
                FA[i] = piece_a
                FB[i] = piece_b
            else:
                VA[k - 1, i] = piece_a.astype(BF16)
                VB[k - 1, i] = piece_b.astype(BF16)

    def video_send(k):
        return [
            send(VA.at[k - 1], RA.at[k - 1], at(dx=k)),
            send(VB.at[k - 1], RB.at[k - 1], at(dy=k)),
        ]

    def caption_part(first):
        return lax.dot_general(
            PR[:, first : first + 512], V[...], (((0,), (0,)), ((), ())),
            preferred_element_type=F32,
        )

    sums = (jnp.zeros((8, 1024), F32),) * 3

    pass_on(0)
    cap_side.wait_recv()
    collect(0)
    sums = pair_step(0, 0, sums)
    own_pairs()
    for i in (1, 3, 2):
        pass_on(i)
    for k in (1, 3):
        collect(k)
        sums = pair_step(k, 0, sums)
    cap_up.wait_recv()
    relay_up = send(C.at[1024:1280], C.at[1536:1792], at(other=True))
    cap_down.wait_recv()
    relay_down = send(C.at[1280:1536], C.at[1792:2048], at(other=True))
    relay_up.wait_recv()
    relay_down.wait_recv()
    first = []
    for k in (1, 3):
        sums = pair_step(k, 1, sums)
        video_step(k)
        first += video_send(k)
    for copy in far:
        copy.wait_recv()
    collect(2)
    for half in (0, 1):
        sums = pair_step(2, half, sums)
    video_step(2)
    first += video_send(2)
    sums = pair_step(0, 1, sums)

    row_of = lax.broadcasted_iota(jnp.int32, (8, 128), 0)
    SC[0] = jnp.where(
        row_of == 0,
        jnp.sum(sums[1]) - SC[21],
        jnp.where(row_of == 1, jnp.sum(sums[2]) - SC[22], jnp.sum(sums[0]) - SC[20]),
    )

    def scalar_send(stage, first_slot, devices):
        return [
            send(SC.at[stage], SC.at[first_slot + n], device) for n, device in enumerate(devices)
        ]

    def scalar_take(stage, first_slot, copies):
        value = SC[stage]
        for n, copy in enumerate(copies):
            copy.wait_recv()
            value = value + SC[first_slot + n]
        SC[stage + 1] = value

    sc_x = scalar_send(0, 8, [at(dx=i) for i in (1, 2, 3)])

    TN1[...] = caption_part(1536).astype(BF16)
    side_near = send(TN1, RN1, at(other=True))
    near = caption_part(1024)
    side_near.wait_recv()
    TN2[...] = (near + RN1[...].astype(F32)).astype(BF16)
    back_down = send(TN2.at[0:256], RN2.at[0:256], at(dz=-1))
    back_up = send(TN2.at[256:512], RN2.at[256:512], at(dz=1))
    scalar_take(0, 8, sc_x)
    sc_y = scalar_send(1, 11, [at(dy=i) for i in (1, 2, 3)])
    video_step(0)

    for copy in first:
        copy.wait_recv()
    for i in range(4):
        for n, (ref, more) in enumerate(((FA, RA), (FB, RB))):
            value = ref[i] + more[0, i].astype(F32) + more[1, i].astype(F32) + more[2, i].astype(F32)
            ref[i] = value
            TP[n, i] = value.astype(BF16)
    second_a, second_b = [], []
    for i in (1, 3, 2):
        second_a.append(send(TP.at[0, (y + i) % 4], RP.at[0, i - 1], at(dy=i)))
        second_b.append(send(TP.at[1, (x + i) % 4], RP.at[1, i - 1], at(dx=i)))
    scalar_take(1, 11, sc_y)
    sc_z = scalar_send(2, 14, [at(dz=2 * i) for i in (1, 2, 3)])
    TS[...] = caption_part(512).astype(BF16)
    side = send(TS, RS, at(other=True))

    for copy in second_a + second_b:
        copy.wait_recv()
    sum_a = FA[y] + RP[0, 0].astype(F32) + RP[0, 1].astype(F32) + RP[0, 2].astype(F32)
    sum_b = FB[x] + RP[1, 0].astype(F32) + RP[1, 1].astype(F32) + RP[1, 2].astype(F32)
    for i, value in enumerate((sum_a[0:16], sum_a[16:32], sum_b[0:16], sum_b[16:32])):
        S2[i] = value
        TZ[i] = value.astype(BF16)
    third = [send(TZ.at[(zh + i) % 4], RZ.at[i - 1], at(dz=2 * i)) for i in (1, 2, 3)]
    scalar_take(2, 14, sc_z)
    sc_p = scalar_send(3, 17, [device_at(x, y, zh * 2 + 1 - zp, core)])
    CG[...] = caption_part(0)
    scalar_take(3, 17, sc_p)
    sc_c = scalar_send(4, 18, [at(other=True)])

    for copy in third:
        copy.wait_recv()
    wide = videos[...].astype(F32)
    video_scale = lax.rsqrt(jnp.sum(wide * wide, axis=1, keepdims=True) + 1e-06)
    unit = wide * video_scale
    grad = temper * (
        S2[zh] + RZ[0].astype(F32) + RZ[1].astype(F32) + RZ[2].astype(F32)
    )
    video_out[...] = video_scale * (grad - unit * jnp.sum(unit * grad, axis=1, keepdims=True))

    scalar_take(4, 18, sc_c)
    scale_of = jnp.where(row_of == 1, jnp.broadcast_to(temper, (8, 128)), 1.0)
    scalar_out[...] = SC[5] * scale_of * (1.0 / 536870912.0)

    side.wait_recv()
    back_down.wait_recv()
    back_up.wait_recv()

    def finish(i, carry):
        rows = pl.ds(pl.multiple_of(i * 64, 64), 64)
        block = captions[rows, :].astype(F32)
        scale = lax.rsqrt(jnp.sum(block * block, axis=1, keepdims=True) + 1e-06)
        unit = block * scale
        grad = temper * (CG[rows, :] + RS[rows, :].astype(F32) + RN2[rows, :].astype(F32))
        caption_out[rows, :] = scale * (grad - unit * jnp.sum(unit * grad, axis=1, keepdims=True))
        return carry

    lax.fori_loop(0, CAP // 64, finish, 0)
    for copy in started:
        copy.wait_send()


def hand_out(video_grad, caption_grad, scalars, video_out, caption_out, scalar_out, sem):
    copies = [pltpu.make_async_copy(video_grad, video_out, sem.at[8])]
    for i in range(8):
        rows = pl.ds(i * (CAP // 8), CAP // 8)
        copies.append(
            pltpu.make_async_copy(caption_grad.at[rows], caption_out.at[rows], sem.at[i])
        )
    for copy in copies:
        copy.start()
    for i in range(3):
        scalar_out[i] = scalars[i, 0]
    for copy in copies:
        copy.wait()


def on_device(videos, captions, caption_owner, log_temp, bias):
    vmem = pl.BlockSpec(memory_space=pltpu.VMEM)
    smem = pl.BlockSpec(memory_space=pltpu.SMEM)
    hbm = pl.BlockSpec(memory_space=pltpu.HBM)
    V = pltpu.VMEM
    video_grad, caption_grad, scalars = pl.pallas_call(
        kernel,
        out_shape=(
            pltpu.VMEM((OWN, D), F32),
            pltpu.VMEM((CAP, D), F32),
            pltpu.VMEM((8, 128), F32),
        ),
        in_specs=[hbm, hbm, hbm, smem, smem],
        out_specs=(vmem, vmem, vmem),
        scratch_shapes=[
            V((4, 4, 64, D), BF16),
            V((ALL, D), BF16),
            V((1024, D), BF16),
            V((1024, ALL), BF16),
            V((3, 4, 32, D), BF16),
            V((3, 4, 32, D), BF16),
            V((4, 32, D), F32),
            V((4, 32, D), F32),
            V((3, 4, 32, D), BF16),
            V((3, 4, 32, D), BF16),
            V((2, 4, 32, D), BF16),
            V((2, 3, 32, D), BF16),
            V((4, OWN, D), F32),
            V((4, OWN, D), BF16),
            V((3, OWN, D), BF16),
            V((CAP, D), BF16),
            V((CAP, D), BF16),
            V((CAP, D), BF16),
            V((CAP, D), BF16),
            V((CAP, D), BF16),
            V((CAP, D), BF16),
            V((CAP, D), F32),
            V((23, 8, 128), F32),
            V((OWN, D), BF16),
            V((CAP, D), BF16),
            V((1, CAP), jnp.int32),
            pltpu.SemaphoreType.DMA((COPIES,)),
            pltpu.SemaphoreType.DMA((COPIES,)),
            pltpu.SemaphoreType.DMA((9,)),
        ],
        compiler_params=pltpu.CompilerParams(
            collective_id=0, has_side_effects=True, vmem_limit_bytes=61 * 2**20
        ),
        cost_estimate=pl.CostEstimate(
            flops=3 * 2 * 1024 * ALL * D, bytes_accessed=4 * 2**20, transcendentals=3 * 1024 * ALL
        ),
    )(
        pltpu.with_memory_space_constraint(videos, pltpu.HBM),
        pltpu.with_memory_space_constraint(captions, pltpu.HBM),
        pltpu.with_memory_space_constraint(caption_owner.reshape(1, CAP), pltpu.HBM),
        log_temp,
        bias,
    )
    video_grad, caption_grad, scalars = pl.pallas_call(
        hand_out,
        out_shape=(
            pltpu.HBM((OWN, D), F32),
            pltpu.HBM((CAP, D), F32),
            jax.ShapeDtypeStruct((3,), F32),
        ),
        in_specs=[vmem, vmem, smem],
        out_specs=(hbm, hbm, smem),
        scratch_shapes=[pltpu.SemaphoreType.DMA((9,))],
    )(video_grad, caption_grad, scalars)
    return video_grad, caption_grad, scalars


def solution(mesh):
    in_specs = (P(("outer", "dp"), None), P(("outer", "dp"), None), P(("outer", "dp")), P(), P())
    out_specs = (P(("outer", "dp"), None), P(("outer", "dp"), None), P())
    return jax.shard_map(
        on_device, mesh=mesh, in_specs=in_specs, out_specs=out_specs, check_vma=False
    )
```

```python
import jax
import jax.numpy as jnp
from jax import lax
from jax.experimental import pallas as pl
from jax.experimental.pallas import tpu as pltpu
from jax.sharding import PartitionSpec as P

MESH = pl.DeviceIdType.MESH
F32 = jnp.float32
BF16 = jnp.bfloat16
LOG2E = 1.4426950408889634
D = 1024
OWN = 16
CAP = 512
ALL = 4 * CAP
COPIES = 96


def device_at(x, y, z, core):
    return ((x // 2) * 2 + core, (y * 2 + x % 2) * 8 + z)


def kernel(
    videos_far, captions_far, owner_far, log_temp, bias,
    video_out, caption_out, scalar_out,
    G, C, V, PR, VA, VB, FA, FB,
    RA, RB, TP, RP, S2, TZ, RZ,
    TN1, RN1, TN2, RN2, TS, RS, CG, SC,
    videos, captions, owner, send_sem, recv_sem, local_sem,
):
    outer, inner = lax.axis_index("outer"), lax.axis_index("dp")
    x = (outer // 2) * 2 + (inner // 8) % 2
    y = inner // 16
    z = inner % 8
    core = outer % 2
    zh, zp = z // 2, z % 2

    def at(dx=0, dy=0, dz=0, other=False):
        return device_at(
            (x + dx + 4) % 4, (y + dy + 4) % 4, (z + dz + 8) % 8, 1 - core if other else core
        )

    started = []

    def send(src, dst, device):
        index = len(started)
        copy = pltpu.make_async_remote_copy(
            src_ref=src, dst_ref=dst, send_sem=send_sem.at[index], recv_sem=recv_sem.at[index],
            device_id=device, device_id_type=MESH,
        )
        copy.start()
        started.append(copy)
        return copy

    partners = [at(dx=i) for i in (1, 2, 3)] + [at(dy=i) for i in (1, 2, 3)]
    partners += [at(dz=i) for i in (1, 2, 4, 6, 7)] + [at(other=True)]
    barrier = pltpu.get_barrier_semaphore()
    for device in partners:
        pl.semaphore_signal(barrier, inc=1, device_id=device, device_id_type=MESH)

    bring_videos = pltpu.make_async_copy(videos_far, videos, local_sem.at[8])
    bring_videos.start()
    bring = []
    for i in range(4):
        rows = pl.ds(i * 128, 128)
        bring.append(
            pltpu.make_async_copy(captions_far.at[rows], captions.at[rows], local_sem.at[i])
        )
    bring.append(pltpu.make_async_copy(owner_far, owner, local_sem.at[7]))
    for copy in bring:
        copy.start()
    temper = jnp.exp(jnp.full((1, 1), log_temp[0], F32))
    bias_value = bias[0]

    bring_videos.wait()
    wide = videos[...].astype(F32)
    video_scale = lax.rsqrt(jnp.sum(wide * wide, axis=1, keepdims=True) + 1e-06)
    own_rows = pl.ds(pl.multiple_of(zh * OWN, OWN), OWN)
    G[x, y, own_rows, :] = (wide * video_scale).astype(BF16)

    pl.semaphore_wait(barrier, len(partners))

    mine = G.at[x, y, own_rows]
    along_z = [send(mine, mine, at(dz=2 * i)) for i in (1, 2, 3)]
    def low_captions(i, carry):
        rows = pl.ds(pl.multiple_of(i * 128, 128), 128)
        block = captions[rows, :].astype(F32)
        scale = lax.rsqrt(jnp.sum(block * block, axis=1, keepdims=True) + 1e-06)
        C[rows, :] = (block * scale).astype(BF16)
        return carry

    for copy in bring:
        copy.wait()
    lax.fori_loop(0, CAP // 128, low_captions, 0)
    cap_up = send(C.at[0:256], C.at[1024:1280], at(dz=1))
    cap_down = send(C.at[256:512], C.at[1280:1536], at(dz=-1))
    cap_side = send(C.at[0:512], C.at[512:1024], at(other=True))
    for copy in along_z:
        copy.wait_recv()

    def unit_a(px, py, lo=0, hi=32):
        return G.at[(px + 4) % 4, (py + 4) % 4, lo:hi]

    def unit_b(px, py, lo=32, hi=64):
        return G.at[(px + 4) % 4, (py + 4) % 4, lo:hi]

    def same(unit, device):
        return send(unit, unit, device)

    ax_p, ax_m, by_p, by_m = {}, {}, {}, {}
    a_y, b_x = {}, {}
    for i in (2, 1, 3):
        a_y[i] = same(unit_a(x, y), at(dy=i))
        b_x[i] = same(unit_b(x, y), at(dx=i))
    ax_p[0] = same(unit_a(x, y), at(dx=1))
    by_p[0] = same(unit_b(x, y), at(dy=1))
    ax_m[0] = same(unit_a(x, y), at(dx=-1))
    by_m[0] = same(unit_b(x, y), at(dy=-1))
    for i in (1, 3, 2):
        a_y[i].wait_recv()
        ax_p[i] = same(unit_a(x, y - i), at(dx=1))
        ax_m[i] = same(unit_a(x, y - i), at(dx=-1))
        b_x[i].wait_recv()
        by_p[i] = same(unit_b(x - i, y), at(dy=1))
        by_m[i] = same(unit_b(x - i, y), at(dy=-1))
    far = []

    def pass_on(i):
        ax_p[i].wait_recv()
        far.append(same(unit_a(x - 1, y - i, 0, 16), at(dx=1)))
        ax_m[i].wait_recv()
        far.append(same(unit_a(x + 1, y - i, 16, 32), at(dx=-1)))
        by_p[i].wait_recv()
        far.append(same(unit_b(x - i, y - 1, 32, 48), at(dy=1)))
        by_m[i].wait_recv()
        far.append(same(unit_b(x - i, y + 1, 48, 64), at(dy=-1)))

    slope = temper * LOG2E
    offset = bias_value * LOG2E

    def collect(k):
        xk, yk = (x + k) % 4, (y + k) % 4
        for i in range(4):
            V[k * 256 + i * 32 : k * 256 + i * 32 + 32, :] = G[xk, i, 0:32, :]
            V[k * 256 + 128 + i * 32 : k * 256 + 128 + i * 32 + 32, :] = G[i, yk, 32:64, :]

    def pair_step(k, half, sums):
        total, logs, power = sums
        rows = slice(k * 256, k * 256 + 256)
        cols = slice(half * 1024, half * 1024 + 1024)
        dots = lax.dot_general(
            V[rows, :], C[cols, :], (((1,), (1,)), ((), ())), preferred_element_type=F32
        )
        grown = jnp.exp2(dots * slope + offset)
        above = 1.0 + grown
        pairs = grown * pl.reciprocal(above, approx=False)
        PR[rows, cols] = pairs.astype(BF16)
        total = total + jnp.sum(pairs.reshape(32, 8, 1024), axis=0)
        quads = above.reshape(8, 4, 8, 1024)
        quads = (quads[:, 0] * quads[:, 1]) * (quads[:, 2] * quads[:, 3])
        logs = logs + jnp.sum(jnp.log(quads), axis=0)
        power = power + jnp.sum((pairs * dots).reshape(32, 8, 1024), axis=0)
        return total, logs, power

    def own_pairs():
        dots = lax.dot_general(
            G[x, y, own_rows, :], C[0:512, :], (((1,), (1,)), ((), ())), preferred_element_type=F32
        )
        grown = jnp.exp2(dots * slope + offset)
        part = pl.reciprocal(1.0 + grown, approx=False)
        first = (outer * 64 + inner) * OWN
        ids = first + lax.broadcasted_iota(jnp.int32, (OWN, CAP), 0)
        match = owner[...] == ids
        pairs = jnp.where(match, -part, grown * part)
        row = jnp.where(zh < 2, y * 32 + zh * 16, 128 + x * 32 + (zh - 2) * 16)
        PR[pl.ds(pl.multiple_of(row, 16), 16), 0:512] = pairs.astype(BF16)
        logits = dots * temper + bias_value
        ones = jnp.where(match, 1.0, 0.0)
        taken = jnp.where(match, logits, 0.0)
        SC[20] = jnp.full((8, 128), jnp.sum(ones), F32)
        SC[21] = jnp.full((8, 128), jnp.sum(taken), F32)
        SC[22] = jnp.full((8, 128), jnp.sum(jnp.where(match, dots, 0.0)), F32)

    def video_step(k):
        part = jnp.dot(PR[k * 256 : k * 256 + 256, :], C[...], preferred_element_type=F32)
        for i in range(4):
            piece_a = part[i * 32 : i * 32 + 32]
            piece_b = part[128 + i * 32 : 128 + i * 32 + 32]
            if k == 0:
                FA[i] = piece_a
                FB[i] = piece_b
            else:
                VA[k - 1, i] = piece_a.astype(BF16)
                VB[k - 1, i] = piece_b.astype(BF16)

    def video_send(k):
        return [
            send(VA.at[k - 1], RA.at[k - 1], at(dx=k)),
            send(VB.at[k - 1], RB.at[k - 1], at(dy=k)),
        ]

    def caption_part(first):
        return lax.dot_general(
            PR[:, first : first + 512], V[...], (((0,), (0,)), ((), ())),
            preferred_element_type=F32,
        )

    sums = (jnp.zeros((8, 1024), F32),) * 3

    pass_on(0)
    cap_side.wait_recv()
    collect(0)
    sums = pair_step(0, 0, sums)
    own_pairs()
    for i in (1, 3, 2):
        pass_on(i)
    for k in (1, 3):
        collect(k)
        sums = pair_step(k, 0, sums)
    cap_up.wait_recv()
    relay_up = send(C.at[1024:1280], C.at[1536:1792], at(other=True))
    cap_down.wait_recv()
    relay_down = send(C.at[1280:1536], C.at[1792:2048], at(other=True))
    relay_up.wait_recv()
    relay_down.wait_recv()
    first = []
    for k in (1, 3):
        sums = pair_step(k, 1, sums)
        video_step(k)
        first += video_send(k)
    for copy in far:
        copy.wait_recv()
    collect(2)
    for half in (0, 1):
        sums = pair_step(2, half, sums)
    video_step(2)
    first += video_send(2)
    sums = pair_step(0, 1, sums)

    row_of = lax.broadcasted_iota(jnp.int32, (8, 128), 0)
    SC[0] = jnp.where(
        row_of == 0,
        jnp.sum(sums[1]) - SC[21],
        jnp.where(row_of == 1, jnp.sum(sums[2]) - SC[22], jnp.sum(sums[0]) - SC[20]),
    )

    def scalar_send(stage, first_slot, devices):
        return [
            send(SC.at[stage], SC.at[first_slot + n], device) for n, device in enumerate(devices)
        ]

    def scalar_take(stage, first_slot, copies):
        value = SC[stage]
        for n, copy in enumerate(copies):
            copy.wait_recv()
            value = value + SC[first_slot + n]
        SC[stage + 1] = value

    sc_z = scalar_send(0, 8, [at(dz=2 * i) for i in (1, 2, 3)])

    TN1[...] = caption_part(1536).astype(BF16)
    side_near = send(TN1, RN1, at(other=True))
    CG[...] = caption_part(1024)
    video_step(0)
    scalar_take(0, 8, sc_z)
    sc_p = scalar_send(1, 11, [device_at(x, y, zh * 2 + 1 - zp, core)])
    side_near.wait_recv()
    TN2[...] = (CG[...] + RN1[...].astype(F32)).astype(BF16)
    back_down = send(TN2.at[0:256], RN2.at[0:256], at(dz=-1))
    back_up = send(TN2.at[256:512], RN2.at[256:512], at(dz=1))

    second = []
    for n, (ref, more) in enumerate(((FA, RA), (FB, RB))):
        for copy in first[n::2]:
            copy.wait_recv()
        for i in range(4):
            value = ref[i] + more[0, i].astype(F32) + more[1, i].astype(F32) + more[2, i].astype(F32)
            ref[i] = value
            TP[n, i] = value.astype(BF16)
        for i in (2, 1, 3):
            if n == 0:
                second.append(send(TP.at[0, (y + i) % 4], RP.at[0, i - 1], at(dy=i)))
            else:
                second.append(send(TP.at[1, (x + i) % 4], RP.at[1, i - 1], at(dx=i)))
    scalar_take(1, 11, sc_p)
    sc_c = scalar_send(2, 12, [at(other=True)])
    TS[...] = caption_part(512).astype(BF16)
    side = send(TS, RS, at(other=True))

    for copy in second:
        copy.wait_recv()
    sum_a = FA[y] + RP[0, 0].astype(F32) + RP[0, 1].astype(F32) + RP[0, 2].astype(F32)
    sum_b = FB[x] + RP[1, 0].astype(F32) + RP[1, 1].astype(F32) + RP[1, 2].astype(F32)
    for i, value in enumerate((sum_a[0:16], sum_a[16:32], sum_b[0:16], sum_b[16:32])):
        S2[i] = value
        TZ[i] = value.astype(BF16)
    third = [send(TZ.at[(zh + i) % 4], RZ.at[i - 1], at(dz=2 * i)) for i in (1, 2, 3)]
    scalar_take(2, 12, sc_c)
    sc_x = scalar_send(3, 13, [at(dx=i) for i in (1, 2, 3)])
    CG[...] = caption_part(0)
    scalar_take(3, 13, sc_x)
    sc_y = scalar_send(4, 16, [at(dy=i) for i in (1, 2, 3)])

    for copy in third:
        copy.wait_recv()
    wide = videos[...].astype(F32)
    video_scale = lax.rsqrt(jnp.sum(wide * wide, axis=1, keepdims=True) + 1e-06)
    unit = wide * video_scale
    grad = temper * (
        S2[zh] + RZ[0].astype(F32) + RZ[1].astype(F32) + RZ[2].astype(F32)
    )
    video_out[...] = video_scale * (grad - unit * jnp.sum(unit * grad, axis=1, keepdims=True))

    scalar_take(4, 16, sc_y)
    scale_of = jnp.where(row_of == 1, jnp.broadcast_to(temper, (8, 128)), 1.0)
    scalar_out[...] = SC[5] * scale_of * (1.0 / 536870912.0)

    side.wait_recv()
    back_down.wait_recv()
    back_up.wait_recv()

    def finish(i, carry):
        rows = pl.ds(pl.multiple_of(i * 64, 64), 64)
        block = captions[rows, :].astype(F32)
        scale = lax.rsqrt(jnp.sum(block * block, axis=1, keepdims=True) + 1e-06)
        unit = block * scale
        grad = temper * (CG[rows, :] + RS[rows, :].astype(F32) + RN2[rows, :].astype(F32))
        caption_out[rows, :] = scale * (grad - unit * jnp.sum(unit * grad, axis=1, keepdims=True))
        return carry

    lax.fori_loop(0, CAP // 64, finish, 0)
    for copy in started:
        copy.wait_send()


def hand_out(video_grad, caption_grad, scalars, video_out, caption_out, scalar_out, sem):
    copies = [pltpu.make_async_copy(video_grad, video_out, sem.at[8])]
    for i in range(8):
        rows = pl.ds(i * (CAP // 8), CAP // 8)
        copies.append(
            pltpu.make_async_copy(caption_grad.at[rows], caption_out.at[rows], sem.at[i])
        )
    for copy in copies:
        copy.start()
    for i in range(3):
        scalar_out[i] = scalars[i, 0]
    for copy in copies:
        copy.wait()


def on_device(videos, captions, caption_owner, log_temp, bias):
    vmem = pl.BlockSpec(memory_space=pltpu.VMEM)
    smem = pl.BlockSpec(memory_space=pltpu.SMEM)
    hbm = pl.BlockSpec(memory_space=pltpu.HBM)
    V = pltpu.VMEM
    video_grad, caption_grad, scalars = pl.pallas_call(
        kernel,
        out_shape=(
            pltpu.VMEM((OWN, D), F32),
            pltpu.VMEM((CAP, D), F32),
            pltpu.VMEM((8, 128), F32),
        ),
        in_specs=[hbm, hbm, hbm, smem, smem],
        out_specs=(vmem, vmem, vmem),
        scratch_shapes=[
            V((4, 4, 64, D), BF16),
            V((ALL, D), BF16),
            V((1024, D), BF16),
            V((1024, ALL), BF16),
            V((3, 4, 32, D), BF16),
            V((3, 4, 32, D), BF16),
            V((4, 32, D), F32),
            V((4, 32, D), F32),
            V((3, 4, 32, D), BF16),
            V((3, 4, 32, D), BF16),
            V((2, 4, 32, D), BF16),
            V((2, 3, 32, D), BF16),
            V((4, OWN, D), F32),
            V((4, OWN, D), BF16),
            V((3, OWN, D), BF16),
            V((CAP, D), BF16),
            V((CAP, D), BF16),
            V((CAP, D), BF16),
            V((CAP, D), BF16),
            V((CAP, D), BF16),
            V((CAP, D), BF16),
            V((CAP, D), F32),
            V((23, 8, 128), F32),
            V((OWN, D), BF16),
            V((CAP, D), BF16),
            V((1, CAP), jnp.int32),
            pltpu.SemaphoreType.DMA((COPIES,)),
            pltpu.SemaphoreType.DMA((COPIES,)),
            pltpu.SemaphoreType.DMA((9,)),
        ],
        compiler_params=pltpu.CompilerParams(
            collective_id=0, has_side_effects=True, vmem_limit_bytes=61 * 2**20
        ),
        cost_estimate=pl.CostEstimate(
            flops=3 * 2 * 1024 * ALL * D, bytes_accessed=4 * 2**20, transcendentals=3 * 1024 * ALL
        ),
    )(
        pltpu.with_memory_space_constraint(videos, pltpu.HBM),
        pltpu.with_memory_space_constraint(captions, pltpu.HBM),
        pltpu.with_memory_space_constraint(caption_owner.reshape(1, CAP), pltpu.HBM),
        log_temp,
        bias,
    )
    video_grad, caption_grad, scalars = pl.pallas_call(
        hand_out,
        out_shape=(
            pltpu.HBM((OWN, D), F32),
            pltpu.HBM((CAP, D), F32),
            jax.ShapeDtypeStruct((3,), F32),
        ),
        in_specs=[vmem, vmem, smem],
        out_specs=(hbm, hbm, smem),
        scratch_shapes=[pltpu.SemaphoreType.DMA((9,))],
    )(video_grad, caption_grad, scalars)
    return video_grad, caption_grad, scalars


def solution(mesh):
    in_specs = (P(("outer", "dp"), None), P(("outer", "dp"), None), P(("outer", "dp")), P(), P())
    out_specs = (P(("outer", "dp"), None), P(("outer", "dp"), None), P())
    return jax.shard_map(
        on_device, mesh=mesh, in_specs=in_specs, out_specs=out_specs, check_vma=False
    )
```
